32 devices in a mesh: group: 2 (over y), row: 4 (over z), col: 4 (over x, core).
Axes of the slice: x: 2, y: 2, z: 4, core: 2. Of those that a mesh axis runs over, the one named last changes fastest.
Arguments:
- pair: bfloat16 [1024, 512, 128], P(('group', 'row'), 'col'), parts along dimension 0, may hold values from -6 to 6
- chain_ids: int32 [1024], P('group'), parts along dimension 0, may hold values from 0 to 5, never falling along the last dimension, each value on 1 to 256 neighbouring positions
- block_mask: int32 [8, 4], P('group'), parts along dimension 0, may hold values 0 or 1
- norm_gain: float32 [2, 128], replicated, may hold values from 0.1 to 1.9
- norm_bias: float32 [2, 128], replicated, may hold values from -3 to 3
- proj_weight: bfloat16 [2, 128, 512], replicated, may hold values from -0.5 to 0.5
- gate_weight: bfloat16 [2, 128, 128], replicated, may hold values from -0.5 to 0.5
- out_gain: float32 [2, 128], replicated, may hold values from 0.1 to 1.9
- out_bias: float32 [2, 128], replicated, may hold values from -3 to 3
- out_weight: bfloat16 [2, 128, 128], replicated, may hold values from -0.5 to 0.5
Outputs:
- updated: bfloat16 [1024, 512, 128], P(('group', 'row'), 'col'), parts along dimension 0
The draws below stay inside these ranges and needn't reach their ends.
There are 2 independent parts, one for each index of `group`. The reference program is written for one: setup_inputs(seed, part) draws one part's arguments, and reference() takes and returns one part's arrays. A program takes and returns all parts, laid end to end along the dimension named above; an argument that names none is the same for every part. Nothing has to cross between parts.
Inputs may be any that keep to these rules, and one draw needn't show every extreme that they name: `chain_ids`: chain ids never fall along the tokens; each chain holds 1 to 256 tokens, one chain exactly 256.
All inputs are finite; a program needn't handle non-finite values.
Results may differ from the reference program's by a relative error of at most 0.0095.
Values may be sent and summed in bfloat16 or wider, within the bound.
A program may use at most 192 MiB of HBM per device.

```python
import math
import jax
import jax.numpy as jnp
import numpy as np
from jax import lax

TOKENS = 512
PAIR = 128
HIDDEN_SIZE = 128
BLOCK = 128
CHAINS = 6
BLOCKS = 4


def set_ends(drawn, stream_key, least, top_value):
    spot = [jax.random.randint(jax.random.fold_in(stream_key, axis), (), 0, length) for axis, length in enumerate(drawn.shape)]
    widest = drawn.shape.index(max(drawn.shape))
    neighbour = spot[:widest] + [(spot[widest] + 1) % drawn.shape[widest]] + spot[widest + 1:]
    return drawn.at[tuple(spot)].set(least).at[tuple(neighbour)].set(top_value)


def levels(own_key, shape, split, low, top_value):
    def one(dim, blocks):
        heights = jax.random.uniform(jax.random.fold_in(jax.random.fold_in(own_key, 6), dim), (blocks,), jnp.float32, low / len(split), top_value / len(split))
        return jnp.repeat(jnp.exp(heights), shape[dim] // blocks).reshape((-1,) + (1,) * (len(shape) - dim - 1))

    loudness = one(*split[0])
    for cut in split[1:]:
        loudness = loudness * one(*cut)
    return loudness


def split_up(number_of, total, bound, lean):
    weights = [(1 << 20) // math.isqrt(rank ** lean) + 1 for rank in range(2, number_of + 1)]
    spare, given = total - bound - (number_of - 1), [1] * (number_of - 1)
    while spare > 0:
        movable = [i for i in range(number_of - 1) if given[i] < bound]
        mass, budget = sum([weights[i] for i in movable]), spare
        for i in movable:
            extra = min(bound - given[i], max(1, budget * weights[i] // mass), spare)
            given[i] = given[i] + extra
            spare = spare - extra
    return np.array([bound] + given)


def uneven_parts(own_key, amount, total, most, skew):
    if amount == 2:
        one = jax.random.randint(own_key, (), max(1, total - most), min(most, total - 1) + 1)
        return jnp.stack([one, total - one])
    tallies = jnp.asarray(split_up(amount, total, most, skew), jnp.int32)
    pairs = (amount - 1) // 2
    source_of, sink = tallies[1:1 + 2 * pairs:2], tallies[2:2 + 2 * pairs:2]
    slack = jnp.minimum(source_of - 1, most - sink)
    moved = jax.random.randint(jax.random.fold_in(own_key, 1), (pairs,), 0, 1 << 20) % (slack + 1)
    tallies = tallies.at[1:1 + 2 * pairs:2].set(source_of - moved).at[2:2 + 2 * pairs:2].set(sink + moved)
    return tallies[jax.random.permutation(jax.random.fold_in(own_key, 2), amount)]


def normal_values(key, dims, scale, limit, split=(), held_as=jnp.bfloat16):
    drawn = jax.random.normal(key, dims, jnp.float32) * scale
    if len(split) > 0:
        drawn = levels(key, dims, split, -0.22, 0.18) * drawn
    return jnp.clip(drawn, min=-limit, max=limit).astype(held_as)


def setup_inputs(seed: int = 0, part: int = 0) -> dict:
    splits = jax.random.split(jax.random.key(seed), 11)
    part_splits = jax.random.split(jax.random.fold_in(splits[10], part), 11)
    return {
        "pair": normal_values(part_splits[0], (TOKENS, TOKENS, PAIR), 1.0, 6.0, ((0, 4), (1, 4))),
        "chain_ids": jnp.searchsorted(jnp.cumsum(uneven_parts(part_splits[1], CHAINS, TOKENS, TOKENS // 2, 2)), jnp.arange(TOKENS), side="right").astype(jnp.int32),
        "block_mask": set_ends((jax.random.randint(part_splits[2], (BLOCKS, BLOCKS), 0, 4) < 1).astype(jnp.int32), jax.random.fold_in(part_splits[2], 1), 0, 1),
        "norm_gain": jnp.clip(1.0 + 0.18 * jax.random.normal(splits[3], (2, PAIR), jnp.float32), 0.1, 1.9),
        "norm_bias": normal_values(splits[4], (2, PAIR), 0.5, 3.0, (), jnp.float32),
        "proj_weight": normal_values(splits[5], (2, PAIR, 4 * HIDDEN_SIZE), PAIR ** -0.5, 0.5),
        "gate_weight": normal_values(splits[6], (2, PAIR, PAIR), PAIR ** -0.5, 0.5),
        "out_gain": jnp.clip(1.0 + 0.18 * jax.random.normal(splits[7], (2, HIDDEN_SIZE), jnp.float32), 0.1, 1.9),
        "out_bias": normal_values(splits[8], (2, HIDDEN_SIZE), 0.5, 3.0, (), jnp.float32),
        "out_weight": normal_values(splits[9], (2, HIDDEN_SIZE, PAIR), HIDDEN_SIZE ** -0.5, 0.5),
    }


EPSILON = 1e-05

def layer_norm(values, norm_gain, norm_shift):
    center = values - lax.optimization_barrier(jnp.mean(values, axis=-1, keepdims=True))
    spread = lax.optimization_barrier(jnp.mean(center * center, axis=-1, keepdims=True))
    return center * lax.rsqrt(spread + EPSILON) * norm_gain + norm_shift

def run_pass(state, pair_mask, norm_gain, norm_bias, proj_weight, gate_weight, out_gain, out_bias, out_weight, which_pass, outgoing):
    tokens = state.shape[0]
    channels = state.shape[2]
    hidden = out_gain.shape[1]
    widened = state.astype(jnp.float32)
    normed = layer_norm(widened, norm_gain[which_pass], norm_bias[which_pass]).astype(jnp.bfloat16)
    flattened = normed.reshape(tokens * tokens, channels)
    projected = jnp.dot(flattened, proj_weight[which_pass], preferred_element_type=jnp.float32)
    projected = projected.reshape(tokens, tokens, 4 * hidden)
    masked = pair_mask[:, :, None]
    left_side = (masked * jax.nn.sigmoid(projected[:, :, :hidden]) * projected[:, :, hidden:2 * hidden]).astype(jnp.bfloat16)
    right_side = (masked * jax.nn.sigmoid(projected[:, :, 2 * hidden:3 * hidden]) * projected[:, :, 3 * hidden:]).astype(jnp.bfloat16)
    if outgoing:
        triangle = jnp.einsum('ikh,jkh->ijh', left_side.astype(jnp.float32), right_side.astype(jnp.float32), precision=lax.Precision.HIGHEST)
    else:
        triangle = jnp.einsum('kih,kjh->ijh', left_side.astype(jnp.float32), right_side.astype(jnp.float32), precision=lax.Precision.HIGHEST)
    tri_normed = layer_norm(triangle, out_gain[which_pass], out_bias[which_pass]).astype(jnp.bfloat16)
    gating = jax.nn.sigmoid(jnp.dot(flattened, gate_weight[which_pass], preferred_element_type=jnp.float32))
    projected_out = jnp.dot(tri_normed.reshape(tokens * tokens, hidden), out_weight[which_pass], preferred_element_type=jnp.float32)
    update = (gating * projected_out).reshape(tokens, tokens, channels)
    return (widened + update).astype(jnp.bfloat16)

def reference(pair, chain_ids, block_mask, norm_gain, norm_bias, proj_weight, gate_weight, out_gain, out_bias, out_weight):
    block_ids = jnp.arange(TOKENS, dtype=jnp.int32) // BLOCK
    block_full = block_mask[block_ids][:, block_ids].astype(jnp.float32)
    same_chain = (chain_ids[:, None] == chain_ids[None, :]).astype(jnp.float32)
    pair_mask = jnp.maximum(same_chain, block_full)
    middle = run_pass(pair, pair_mask, norm_gain, norm_bias, proj_weight, gate_weight, out_gain, out_bias, out_weight, 0, True)
    return run_pass(middle, pair_mask, norm_gain, norm_bias, proj_weight, gate_weight, out_gain, out_bias, out_weight, 1, False)
```

```python
import functools

import jax
import jax.numpy as jnp
from jax import lax
from jax.experimental import pallas as pl
from jax.experimental.pallas import tpu as pltpu
from jax.sharding import PartitionSpec as P

BLOCK = 128


EPSILON = 1e-05


def layer_norm(values, norm_gain, norm_shift):
    center = values - jnp.mean(values, axis=-1, keepdims=True)
    spread = jnp.mean(center * center, axis=-1, keepdims=True)
    return center * lax.rsqrt(spread + EPSILON) * norm_gain + norm_shift


def mask_tile(chain_ids, block_mask, tile_rows, tile_cols):
    row_start = lax.axis_index("row") * tile_rows
    col_start = lax.axis_index("col") * tile_cols
    row_tokens = row_start + jnp.arange(tile_rows, dtype=jnp.int32)
    col_tokens = col_start + jnp.arange(tile_cols, dtype=jnp.int32)
    row_chain = lax.dynamic_slice_in_dim(chain_ids, row_start, tile_rows)
    col_chain = lax.dynamic_slice_in_dim(chain_ids, col_start, tile_cols)
    block_ids = jnp.arange(block_mask.shape[0], dtype=jnp.int32)
    row_onehot = (row_tokens[:, None] // BLOCK == block_ids[None, :]).astype(jnp.float32)
    col_onehot = (col_tokens[:, None] // BLOCK == block_ids[None, :]).astype(jnp.float32)
    row_blocks = jnp.dot(
        row_onehot, block_mask.astype(jnp.float32), precision=lax.Precision.HIGHEST
    )
    block_tile = jnp.dot(row_blocks, col_onehot.T, precision=lax.Precision.HIGHEST)
    same_chain = (row_chain[:, None] == col_chain[None, :]).astype(jnp.float32)
    return jnp.maximum(same_chain, block_tile)


def panels_outgoing(left_side, right_side):
    tile_cols = left_side.shape[1]
    right_panel = lax.all_gather(right_side, "row", axis=0, tiled=True)

    def partial_sum(offset, amount):
        return jnp.einsum(
            "jkh,ikh->jih", right_panel, left_side, preferred_element_type=jnp.float32
        )

    summed = lax.psum_scatter(
        partial_sum(jnp.int32(0), lax.axis_size("col") * tile_cols).astype(jnp.bfloat16),
        "col",
        scatter_dimension=0,
        tiled=True,
    ).astype(jnp.float32)
    return jnp.transpose(summed, (1, 0, 2))


def panels_incoming(left_side, right_side):
    tile_rows = left_side.shape[0]
    left_panel = lax.all_gather(left_side, "col", axis=1, tiled=True)

    def partial_sum(offset, amount):
        return jnp.einsum(
            "kih,kjh->ijh", left_panel, right_side, preferred_element_type=jnp.float32
        )

    return lax.psum_scatter(
        partial_sum(jnp.int32(0), lax.axis_size("row") * tile_rows).astype(jnp.bfloat16),
        "row",
        scatter_dimension=0,
        tiled=True,
    ).astype(jnp.float32)


MESH = pl.DeviceIdType.MESH
CHUNKS = 8


def triangle_kernel(
    outgoing, half, step, moved_ref, fixed_ref, out_ref, moved, fixed, summed, landed, sent,
    ready, local_sem, send_moved, recv_moved, send_fixed, recv_fixed, send_peer, recv_peer,
    send_relay, recv_relay, send_sum, recv_sum, send_out, recv_out,
):
    row, col = lax.axis_index("row"), lax.axis_index("col")
    side, place = row // 2, row % 2
    across, core = col // 2, col % 2
    hub = (row == 1) | (row == 2)
    edge = jnp.logical_not(hub)
    hub_row = side + 1
    end_row = 3 * side
    end_place = side
    hub_place = 1 - side
    other = 1 - core
    pair_at = {"row": row, "col": 2 * across + other}
    if outgoing:
        slot = (row, core)
        held = (place, core)
        mine = across
        peer = [{"row": 3 - row, "col": 2 * across + b} for b in range(2)]
        peer_same = {"row": 3 - row, "col": col}
        sum_peer = {"row": row, "col": 2 * (1 - across) + core}
        moved_pair, fixed_pair = (row, other), (place, other)
        moved_end = [(end_row, b) for b in range(2)]
        fixed_end = [(end_place, b) for b in range(2)]
        moved_peer = [(3 - row, b) for b in range(2)]
    else:
        slot = (col, place)
        held = (core, place)
        mine = side
        peer = [{"row": row, "col": 2 * (1 - across) + b} for b in range(2)]
        peer_same = {"row": row, "col": 2 * (1 - across) + core}
        sum_peer = {"row": 3 - row, "col": col}
        moved_pair, fixed_pair = (2 * across + other, place), (other, place)
        moved_end = [(2 * across + b, end_place) for b in range(2)]
        fixed_end = [(b, end_place) for b in range(2)]
        moved_peer = [(2 * (1 - across) + b, place) for b in range(2)]
    hub_at = [{"row": hub_row, "col": 2 * across + b} for b in range(2)]
    end_at = [{"row": end_row, "col": 2 * across + b} for b in range(2)]

    def remote(source, target, send, recv, device):
        return pltpu.make_async_remote_copy(
            src_ref=source, dst_ref=target, send_sem=send, recv_sem=recv,
            device_id=device, device_id_type=MESH,
        )

    def part(g):
        return pl.ds(g * step, step)

    def span(half_of, g):
        return pl.ds(half_of * half + g * step, step)

    def swap_moved(g):
        return remote(moved_ref.at[span(other, g)], moved.at[slot[0], slot[1], part(g)],
                      send_moved.at[0, g], recv_moved.at[0, g], pair_at)

    def swap_fixed(g):
        return remote(fixed_ref.at[span(other, g)], fixed.at[held[0], held[1], part(g)],
                      send_fixed.at[0, g], recv_fixed.at[0, g], pair_at)

    def end_moved(g, b):
        return remote(moved_ref.at[span(b, g)], moved.at[slot[0], slot[1], part(g)],
                      send_moved.at[b, g], recv_moved.at[1 + core, g], hub_at[b])

    def end_fixed(g, b):
        return remote(fixed_ref.at[span(b, g)], fixed.at[held[0], held[1], part(g)],
                      send_fixed.at[b, g], recv_fixed.at[1 + core, g], hub_at[b])

    def to_peer(g, b):
        return remote(moved_ref.at[span(b, g)], moved.at[slot[0], slot[1], part(g)],
                      send_peer.at[b, g], recv_peer.at[core, g], peer[b])

    def relay_view(g, there):
        if outgoing:
            return moved.at[3 - end_row if there else end_row, :, part(g)]
        start = 2 * (1 - across if there else across)
        return moved.at[pl.ds(start, 2), end_place, part(g)]

    def relay(g):
        return remote(relay_view(g, False), relay_view(g, False),
                      send_relay.at[g], recv_relay.at[g], peer_same)

    def arrived(view, sem):
        remote(view, view, send_relay.at[0], sem, pair_at).wait_recv()

    def sums_to(g):
        return remote(sent.at[g % 2], landed.at[part(g)], send_sum.at[g], recv_sum.at[g], sum_peer)

    def result_pair(g):
        return remote(ready.at[g % 2, hub_place, other], out_ref.at[span(core, g)],
                      send_out.at[2, g], recv_out.at[core, g], pair_at)

    def result_end(g, b):
        return remote(ready.at[g % 2, end_place, b], out_ref.at[span(core, g)],
                      send_out.at[b, g], recv_out.at[core, g], end_at[b])

    barrier = pltpu.get_barrier_semaphore()

    @pl.when(hub)
    def _():
        for device in [pair_at, sum_peer] + end_at + peer:
            pl.semaphore_signal(barrier, inc=1, device_id=device, device_id_type=MESH)
        pl.semaphore_wait(barrier, 6)

    @pl.when(edge)
    def _():
        for device in hub_at:
            pl.semaphore_signal(barrier, inc=1, device_id=device, device_id_type=MESH)
        pl.semaphore_wait(barrier, 2)

    def tile(group, e, b, h):
        total = None
        for v in range(2):
            if outgoing:
                lhs, rhs = fixed[e, v, h], moved[2 * group + b, v, h]
            else:
                lhs, rhs = moved[2 * group + e, v, h], fixed[b, v, h]
            term = jnp.dot(lhs, rhs, preferred_element_type=jnp.float32)
            total = term if total is None else total + term
        return total

    @pl.when(edge)
    def _():
        for g in range(CHUNKS):
            if g >= 2:
                for b in range(2):
                    end_moved(g - 2, b).wait_send()
                    end_fixed(g - 2, b).wait_send()
            for b in range(2):
                end_moved(g, b).start()
            for b in range(2):
                end_fixed(g, b).start()
        for g in range(CHUNKS - 2, CHUNKS):
            for b in range(2):
                end_moved(g, b).wait_send()
                end_fixed(g, b).wait_send()
        for g in range(CHUNKS):
            for b in range(2):
                arrived(out_ref.at[span(b, g)], recv_out.at[b, g])

    @pl.when(hub)
    def _():
        own = [
            pltpu.make_async_copy(moved_ref.at[pl.ds(core * half, half)],
                                  moved.at[slot[0], slot[1]], local_sem.at[0]),
            pltpu.make_async_copy(fixed_ref.at[pl.ds(core * half, half)],
                                  fixed.at[held[0], held[1]], local_sem.at[1]),
        ]

        def begin(g):
            for b in range(2):
                to_peer(g, b).start()
            swap_moved(g).start()
            swap_fixed(g).start()

        begin(0)
        for copy in own:
            copy.start()
        begin(1)
        for copy in own:
            copy.wait()
        for g in range(CHUNKS + 2):
            if 2 <= g + 1 < CHUNKS:
                begin(g + 1)
            if g < CHUNKS:
                for b in range(2):
                    u, v = moved_end[b]
                    arrived(moved.at[u, v, part(g)], recv_moved.at[1 + b, g])
                relay(g).start()
            n = g - 1
            if 0 <= n < CHUNKS:
                for b in range(2):
                    u, v = fixed_end[b]
                    arrived(fixed.at[u, v, part(n)], recv_fixed.at[1 + b, n])
                    u, v = moved_peer[b]
                    arrived(moved.at[u, v, part(n)], recv_peer.at[b, n])
                arrived(moved.at[moved_pair[0], moved_pair[1], part(n)], recv_moved.at[0, n])
                arrived(fixed.at[fixed_pair[0], fixed_pair[1], part(n)], recv_fixed.at[0, n])
                arrived(relay_view(n, True), recv_relay.at[n])
                if n >= 2:
                    sums_to(n - 2).wait_send()

                @pl.loop(0, step)
                def _(h):
                    for e in range(2):
                        for b in range(2):
                            sent[n % 2, h, e, b] = tile(1 - mine, e, b, n * step + h).astype(
                                jnp.bfloat16
                            )

                sums_to(n).start()

                @pl.loop(0, step)
                def _(h):
                    for e in range(2):
                        for b in range(2):
                            summed[n % 2, h, e, b] = tile(mine, e, b, n * step + h)

            n = g - 2
            if 0 <= n < CHUNKS:
                arrived(landed.at[part(n)], recv_sum.at[n])
                if n >= 2:
                    result_pair(n - 2).wait_send()
                    for b in range(2):
                        result_end(n - 2, b).wait_send()

                @pl.loop(0, step)
                def _(h):
                    for e in range(2):
                        for b in range(2):
                            ready[n % 2, e, b, h] = (
                                summed[n % 2, h, e, b]
                                + landed[n * step + h, e, b].astype(jnp.float32)
                            ).astype(jnp.bfloat16)
                    out_ref[core * half + n * step + h] = ready[n % 2, hub_place, core, h]

                for b in range(2):
                    result_end(n, b).start()
                result_pair(n).start()
        for g in range(CHUNKS):
            for b in range(2):
                to_peer(g, b).wait_send()
            swap_moved(g).wait_send()
            swap_fixed(g).wait_send()
            relay(g).wait_send()
        for g in range(CHUNKS - 2, CHUNKS):
            sums_to(g).wait_send()
            result_pair(g).wait_send()
            for b in range(2):
                result_end(g, b).wait_send()
        for g in range(CHUNKS):
            arrived(out_ref.at[span(other, g)], recv_out.at[other, g])


def hub_sums(left_side, right_side, outgoing):
    moved, fixed = (right_side, left_side) if outgoing else (left_side, right_side)
    hidden, edge = moved.shape[0], moved.shape[1]
    half = hidden // 2
    step = half // CHUNKS
    tile = (edge, edge)
    sem = pltpu.SemaphoreType.DMA
    return pl.pallas_call(
        functools.partial(triangle_kernel, outgoing, half, step),
        out_shape=jax.ShapeDtypeStruct(moved.shape, jnp.bfloat16),
        in_specs=[pl.BlockSpec(memory_space=pl.ANY)] * 2,
        out_specs=pl.BlockSpec(memory_space=pltpu.VMEM),
        scratch_shapes=[
            pltpu.VMEM((4, 2, half) + tile, jnp.bfloat16),
            pltpu.VMEM((2, 2, half) + tile, jnp.bfloat16),
            pltpu.VMEM((2, step, 2, 2) + tile, jnp.float32),
            pltpu.VMEM((half, 2, 2) + tile, jnp.bfloat16),
            pltpu.VMEM((2, step, 2, 2) + tile, jnp.bfloat16),
            pltpu.VMEM((2, 2, 2, step) + tile, jnp.bfloat16),
            sem((2,)),
            sem((2, CHUNKS)), sem((3, CHUNKS)),
            sem((2, CHUNKS)), sem((3, CHUNKS)),
            sem((2, CHUNKS)), sem((2, CHUNKS)),
            sem((CHUNKS,)), sem((CHUNKS,)),
            sem((CHUNKS,)), sem((CHUNKS,)),
            sem((3, CHUNKS)), sem((2, CHUNKS)),
        ],
        compiler_params=pltpu.CompilerParams(
            collective_id=0 if outgoing else 1,
            has_side_effects=True,
            vmem_limit_bytes=56 * 1024 * 1024,
        ),
        cost_estimate=pl.CostEstimate(
            flops=32 * hidden * edge**3, bytes_accessed=6 * hidden * edge * edge, transcendentals=0
        ),
    )(moved, fixed)


def takes_hubs(left_side):
    rows, cols, hidden = left_side.shape
    return (
        lax.axis_size("row") == 4
        and lax.axis_size("col") == 4
        and rows == cols
        and rows % 128 == 0
        and hidden % (2 * CHUNKS) == 0
    )


def triangle_sums(left_side, right_side, outgoing):
    if takes_hubs(left_side):
        if outgoing:
            left, right = left_side.transpose(2, 0, 1), right_side.transpose(2, 1, 0)
        else:
            left, right = left_side.transpose(2, 1, 0), right_side.transpose(2, 0, 1)
        return hub_sums(left, right, outgoing).transpose(1, 2, 0).astype(jnp.float32)
    if outgoing:
        return panels_outgoing(left_side, right_side)
    return panels_incoming(left_side, right_side)


def run_pass(
    state,
    pair_mask,
    norm_gain,
    norm_bias,
    proj_weight,
    gate_weight,
    out_gain,
    out_bias,
    out_weight,
    which_pass,
    outgoing,
):
    hidden = out_gain.shape[1]
    widened = state.astype(jnp.float32)
    normed = layer_norm(widened, norm_gain[which_pass], norm_bias[which_pass]).astype(jnp.bfloat16)
    projected = jnp.dot(normed, proj_weight[which_pass], preferred_element_type=jnp.float32)
    masked = pair_mask[:, :, None]
    left_side = (
        masked * jax.nn.sigmoid(projected[:, :, :hidden]) * projected[:, :, hidden : 2 * hidden]
    ).astype(jnp.bfloat16)
    right_side = (
        masked
        * jax.nn.sigmoid(projected[:, :, 2 * hidden : 3 * hidden])
        * projected[:, :, 3 * hidden :]
    ).astype(jnp.bfloat16)
    triangle = triangle_sums(left_side, right_side, outgoing)
    tri_normed = layer_norm(triangle, out_gain[which_pass], out_bias[which_pass]).astype(
        jnp.bfloat16
    )
    gating = jax.nn.sigmoid(
        jnp.dot(normed, gate_weight[which_pass], preferred_element_type=jnp.float32)
    )
    update = gating * jnp.dot(
        tri_normed, out_weight[which_pass], preferred_element_type=jnp.float32
    )
    return (widened + update).astype(jnp.bfloat16)


def local(
    pair,
    chain_ids,
    block_mask,
    norm_gain,
    norm_bias,
    proj_weight,
    gate_weight,
    out_gain,
    out_bias,
    out_weight,
):
    tile_rows, tile_cols = (pair.shape[0], pair.shape[1])
    pair_mask = mask_tile(chain_ids, block_mask, tile_rows, tile_cols)
    middle = run_pass(
        pair,
        pair_mask,
        norm_gain,
        norm_bias,
        proj_weight,
        gate_weight,
        out_gain,
        out_bias,
        out_weight,
        0,
        True,
    )
    return run_pass(
        middle,
        pair_mask,
        norm_gain,
        norm_bias,
        proj_weight,
        gate_weight,
        out_gain,
        out_bias,
        out_weight,
        1,
        False,
    )


def solution(mesh):
    placed = (
        P(("group", "row"), "col", None),
        P("group"),
        P("group", None),
        P(),
        P(),
        P(),
        P(),
        P(),
        P(),
        P(),
    )
    return jax.shard_map(
        local,
        mesh=mesh,
        in_specs=placed,
        out_specs=P(("group", "row"), "col", None),
        check_vma=False,
    )
```

```python
import functools

import jax
import jax.numpy as jnp
from jax import lax
from jax.experimental import pallas as pl
from jax.experimental.pallas import tpu as pltpu
from jax.sharding import PartitionSpec as P

BLOCK = 128


EPSILON = 1e-05


def layer_norm(values, norm_gain, norm_shift):
    center = values - jnp.mean(values, axis=-1, keepdims=True)
    spread = jnp.mean(center * center, axis=-1, keepdims=True)
    return center * lax.rsqrt(spread + EPSILON) * norm_gain + norm_shift


def mask_tile(chain_ids, block_mask, tile_rows, tile_cols):
    row_start = lax.axis_index("row") * tile_rows
    col_start = lax.axis_index("col") * tile_cols
    row_tokens = row_start + jnp.arange(tile_rows, dtype=jnp.int32)
    col_tokens = col_start + jnp.arange(tile_cols, dtype=jnp.int32)
    row_chain = lax.dynamic_slice_in_dim(chain_ids, row_start, tile_rows)
    col_chain = lax.dynamic_slice_in_dim(chain_ids, col_start, tile_cols)
    block_ids = jnp.arange(block_mask.shape[0], dtype=jnp.int32)
    row_onehot = (row_tokens[:, None] // BLOCK == block_ids[None, :]).astype(jnp.float32)
    col_onehot = (col_tokens[:, None] // BLOCK == block_ids[None, :]).astype(jnp.float32)
    row_blocks = jnp.dot(
        row_onehot, block_mask.astype(jnp.float32), precision=lax.Precision.HIGHEST
    )
    block_tile = jnp.dot(row_blocks, col_onehot.T, precision=lax.Precision.HIGHEST)
    same_chain = (row_chain[:, None] == col_chain[None, :]).astype(jnp.float32)
    return jnp.maximum(same_chain, block_tile)


def panels_outgoing(left_side, right_side):
    tile_cols = left_side.shape[1]
    right_panel = lax.all_gather(right_side, "row", axis=0, tiled=True)

    def partial_sum(offset, amount):
        return jnp.einsum(
            "jkh,ikh->jih", right_panel, left_side, preferred_element_type=jnp.float32
        )

    summed = lax.psum_scatter(
        partial_sum(jnp.int32(0), lax.axis_size("col") * tile_cols).astype(jnp.bfloat16),
        "col",
        scatter_dimension=0,
        tiled=True,
    ).astype(jnp.float32)
    return jnp.transpose(summed, (1, 0, 2))


def panels_incoming(left_side, right_side):
    tile_rows = left_side.shape[0]
    left_panel = lax.all_gather(left_side, "col", axis=1, tiled=True)

    def partial_sum(offset, amount):
        return jnp.einsum(
            "kih,kjh->ijh", left_panel, right_side, preferred_element_type=jnp.float32
        )

    return lax.psum_scatter(
        partial_sum(jnp.int32(0), lax.axis_size("row") * tile_rows).astype(jnp.bfloat16),
        "row",
        scatter_dimension=0,
        tiled=True,
    ).astype(jnp.float32)


MESH = pl.DeviceIdType.MESH
CHUNKS = 8


def triangle_kernel(
    outgoing, half, step, moved_ref, fixed_ref, out_ref, moved, fixed, summed, landed, sent,
    ready, local_sem, send_moved, recv_moved, send_fixed, recv_fixed, send_peer, recv_peer,
    send_relay, recv_relay, send_sum, recv_sum, send_out, recv_out,
):
    row, col = lax.axis_index("row"), lax.axis_index("col")
    side, place = row // 2, row % 2
    across, core = col // 2, col % 2
    hub = (row == 1) | (row == 2)
    edge = jnp.logical_not(hub)
    hub_row = side + 1
    end_row = 3 * side
    end_place = side
    hub_place = 1 - side
    other = 1 - core
    pair_at = {"row": row, "col": 2 * across + other}
    if outgoing:
        slot = (row, core)
        held = (place, core)
        mine = across
        peer = [{"row": 3 - row, "col": 2 * across + b} for b in range(2)]
        peer_same = {"row": 3 - row, "col": col}
        sum_peer = {"row": row, "col": 2 * (1 - across) + core}
        moved_pair, fixed_pair = (row, other), (place, other)
        moved_end = [(end_row, b) for b in range(2)]
        fixed_end = [(end_place, b) for b in range(2)]
        moved_peer = [(3 - row, b) for b in range(2)]
    else:
        slot = (col, place)
        held = (core, place)
        mine = side
        peer = [{"row": row, "col": 2 * (1 - across) + b} for b in range(2)]
        peer_same = {"row": row, "col": 2 * (1 - across) + core}
        sum_peer = {"row": 3 - row, "col": col}
        moved_pair, fixed_pair = (2 * across + other, place), (other, place)
        moved_end = [(2 * across + b, end_place) for b in range(2)]
        fixed_end = [(b, end_place) for b in range(2)]
        moved_peer = [(2 * (1 - across) + b, place) for b in range(2)]
    hub_at = [{"row": hub_row, "col": 2 * across + b} for b in range(2)]
    end_at = [{"row": end_row, "col": 2 * across + b} for b in range(2)]

    def remote(source, target, send, recv, device):
        return pltpu.make_async_remote_copy(
            src_ref=source, dst_ref=target, send_sem=send, recv_sem=recv,
            device_id=device, device_id_type=MESH,
        )

    def part(g):
        return pl.ds(g * step, step)

    def span(half_of, g):
        return pl.ds(half_of * half + g * step, step)

    def swap_moved(g):
        return remote(moved_ref.at[span(other, g)], moved.at[slot[0], slot[1], part(g)],
                      send_moved.at[0, g], recv_moved.at[0, g], pair_at)

    def swap_fixed(g):
        return remote(fixed_ref.at[span(other, g)], fixed.at[held[0], held[1], part(g)],
                      send_fixed.at[0, g], recv_fixed.at[0, g], pair_at)

    def end_moved(g, b):
        return remote(moved_ref.at[span(b, g)], moved.at[slot[0], slot[1], part(g)],
                      send_moved.at[b, g], recv_moved.at[1 + core, g], hub_at[b])

    def end_fixed(g, b):
        return remote(fixed_ref.at[span(b, g)], fixed.at[held[0], held[1], part(g)],
                      send_fixed.at[b, g], recv_fixed.at[1 + core, g], hub_at[b])

    def to_peer(g, b):
        return remote(moved_ref.at[span(b, g)], moved.at[slot[0], slot[1], part(g)],
                      send_peer.at[b, g], recv_peer.at[core, g], peer[b])

    def relay_view(g, there):
        if outgoing:
            return moved.at[3 - end_row if there else end_row, :, part(g)]
        start = 2 * (1 - across if there else across)
        return moved.at[pl.ds(start, 2), end_place, part(g)]

    def relay(g):
        return remote(relay_view(g, False), relay_view(g, False),
                      send_relay.at[g], recv_relay.at[g], peer_same)

    def arrived(view, sem):
        remote(view, view, send_relay.at[0], sem, pair_at).wait_recv()

    def sums_to(g):
        return remote(sent.at[g % 2], landed.at[part(g)], send_sum.at[g], recv_sum.at[g], sum_peer)

    def result_pair(g):
        return remote(ready.at[g % 2, hub_place, other], out_ref.at[span(core, g)],
                      send_out.at[2, g], recv_out.at[core, g], pair_at)

    def result_end(g, b):
        return remote(ready.at[g % 2, end_place, b], out_ref.at[span(core, g)],
                      send_out.at[b, g], recv_out.at[core, g], end_at[b])

    barrier = pltpu.get_barrier_semaphore()

    @pl.when(hub)
    def _():
        for device in [pair_at, sum_peer] + end_at + peer:
            pl.semaphore_signal(barrier, inc=1, device_id=device, device_id_type=MESH)
        pl.semaphore_wait(barrier, 6)

    @pl.when(edge)
    def _():
        for device in hub_at:
            pl.semaphore_signal(barrier, inc=1, device_id=device, device_id_type=MESH)
        pl.semaphore_wait(barrier, 2)

    def product(lhs, rhs, dims):
        return lax.dot_general(lhs, rhs, (dims, ((), ())), preferred_element_type=jnp.float32)

    def tiles(group, h):
        for e in range(2):
            if outgoing:
                lhs = [fixed[e, v, h] for v in range(2)]
            else:
                lhs = [moved[2 * group + e, v, h].T for v in range(2)]
            for b in range(2):
                if outgoing:
                    terms = [
                        product(lhs[v], moved[2 * group + b, v, h], ((1,), (1,))) for v in range(2)
                    ]
                else:
                    terms = [product(lhs[v], fixed[b, v, h], ((1,), (0,))) for v in range(2)]
                yield e, b, terms[0] + terms[1]

    @pl.when(edge)
    def _():
        for g in range(CHUNKS):
            if g >= 2:
                for b in range(2):
                    end_moved(g - 2, b).wait_send()
                    end_fixed(g - 2, b).wait_send()
            for b in range(2):
                end_moved(g, b).start()
            for b in range(2):
                end_fixed(g, b).start()
        for g in range(CHUNKS - 2, CHUNKS):
            for b in range(2):
                end_moved(g, b).wait_send()
                end_fixed(g, b).wait_send()
        for g in range(CHUNKS):
            for b in range(2):
                arrived(out_ref.at[span(b, g)], recv_out.at[b, g])

    @pl.when(hub)
    def _():
        own = [
            pltpu.make_async_copy(moved_ref.at[pl.ds(core * half, half)],
                                  moved.at[slot[0], slot[1]], local_sem.at[0]),
            pltpu.make_async_copy(fixed_ref.at[pl.ds(core * half, half)],
                                  fixed.at[held[0], held[1]], local_sem.at[1]),
        ]

        def begin(g):
            for b in range(2):
                to_peer(g, b).start()
            swap_moved(g).start()
            swap_fixed(g).start()

        begin(0)
        for copy in own:
            copy.start()
        begin(1)
        for copy in own:
            copy.wait()
        for g in range(CHUNKS + 2):
            if 2 <= g + 1 < CHUNKS:
                begin(g + 1)
            if g < CHUNKS:
                for b in range(2):
                    u, v = moved_end[b]
                    arrived(moved.at[u, v, part(g)], recv_moved.at[1 + b, g])
                relay(g).start()
            n = g - 1
            if 0 <= n < CHUNKS:
                for b in range(2):
                    u, v = fixed_end[b]
                    arrived(fixed.at[u, v, part(n)], recv_fixed.at[1 + b, n])
                    u, v = moved_peer[b]
                    arrived(moved.at[u, v, part(n)], recv_peer.at[b, n])
                arrived(moved.at[moved_pair[0], moved_pair[1], part(n)], recv_moved.at[0, n])
                arrived(fixed.at[fixed_pair[0], fixed_pair[1], part(n)], recv_fixed.at[0, n])
                arrived(relay_view(n, True), recv_relay.at[n])
                if n >= 2:
                    sums_to(n - 2).wait_send()

                @pl.loop(0, step)
                def _(h):
                    for e, b, total in tiles(1 - mine, n * step + h):
                        sent[n % 2, h, e, b] = total.astype(jnp.bfloat16)

                sums_to(n).start()

                @pl.loop(0, step)
                def _(h):
                    for e, b, total in tiles(mine, n * step + h):
                        summed[n % 2, h, e, b] = total

            n = g - 2
            if 0 <= n < CHUNKS:
                arrived(landed.at[part(n)], recv_sum.at[n])
                if n >= 2:
                    result_pair(n - 2).wait_send()
                    for b in range(2):
                        result_end(n - 2, b).wait_send()

                @pl.loop(0, step)
                def _(h):
                    for e in range(2):
                        for b in range(2):
                            ready[n % 2, e, b, h] = (
                                summed[n % 2, h, e, b]
                                + landed[n * step + h, e, b].astype(jnp.float32)
                            ).astype(jnp.bfloat16)
                    out_ref[core * half + n * step + h] = ready[n % 2, hub_place, core, h]

                for b in range(2):
                    result_end(n, b).start()
                result_pair(n).start()
        for g in range(CHUNKS):
            for b in range(2):
                to_peer(g, b).wait_send()
            swap_moved(g).wait_send()
            swap_fixed(g).wait_send()
            relay(g).wait_send()
        for g in range(CHUNKS - 2, CHUNKS):
            sums_to(g).wait_send()
            result_pair(g).wait_send()
            for b in range(2):
                result_end(g, b).wait_send()
        for g in range(CHUNKS):
            arrived(out_ref.at[span(other, g)], recv_out.at[other, g])


def hub_sums(left_side, right_side, outgoing):
    moved, fixed = (right_side, left_side) if outgoing else (left_side, right_side)
    hidden, edge = moved.shape[0], moved.shape[1]
    half = hidden // 2
    step = half // CHUNKS
    tile = (edge, edge)
    sem = pltpu.SemaphoreType.DMA
    return pl.pallas_call(
        functools.partial(triangle_kernel, outgoing, half, step),
        out_shape=jax.ShapeDtypeStruct(moved.shape, jnp.bfloat16),
        in_specs=[pl.BlockSpec(memory_space=pl.ANY)] * 2,
        out_specs=pl.BlockSpec(memory_space=pltpu.VMEM),
        scratch_shapes=[
            pltpu.VMEM((4, 2, half) + tile, jnp.bfloat16),
            pltpu.VMEM((2, 2, half) + tile, jnp.bfloat16),
            pltpu.VMEM((2, step, 2, 2) + tile, jnp.float32),
            pltpu.VMEM((half, 2, 2) + tile, jnp.bfloat16),
            pltpu.VMEM((2, step, 2, 2) + tile, jnp.bfloat16),
            pltpu.VMEM((2, 2, 2, step) + tile, jnp.bfloat16),
            sem((2,)),
            sem((2, CHUNKS)), sem((3, CHUNKS)),
            sem((2, CHUNKS)), sem((3, CHUNKS)),
            sem((2, CHUNKS)), sem((2, CHUNKS)),
            sem((CHUNKS,)), sem((CHUNKS,)),
            sem((CHUNKS,)), sem((CHUNKS,)),
            sem((3, CHUNKS)), sem((2, CHUNKS)),
        ],
        compiler_params=pltpu.CompilerParams(
            collective_id=0 if outgoing else 1,
            has_side_effects=True,
            vmem_limit_bytes=56 * 1024 * 1024,
        ),
        cost_estimate=pl.CostEstimate(
            flops=32 * hidden * edge**3, bytes_accessed=6 * hidden * edge * edge, transcendentals=0
        ),
    )(moved, fixed)


ROWS = 16


def sigmoid(values):
    return 0.5 * jnp.tanh(0.5 * values) + 0.5


def norm_rows(values, gain, shift):
    center = values - jnp.mean(values, axis=-1, keepdims=True)
    spread = jnp.mean(center * center, axis=-1, keepdims=True)
    return center * lax.rsqrt(spread + EPSILON) * gain + shift


def sides_kernel(x_ref, mask_ref, gain_ref, shift_ref, weight_ref, left_ref, right_ref, a_ref, b_ref):
    hidden = left_ref.shape[0]
    for row in range(ROWS):
        normed = norm_rows(x_ref[row].astype(jnp.float32), gain_ref[...], shift_ref[...])
        projected = lax.dot_general(
            weight_ref[...], normed.astype(jnp.bfloat16), (((1,), (1,)), ((), ())),
            preferred_element_type=jnp.float32,
        )
        masked = mask_ref[row : row + 1, :]
        place = pl.ds(row, hidden, stride=ROWS)
        a_ref[place, :] = masked * sigmoid(projected[:hidden]) * projected[hidden : 2 * hidden]
        b_ref[place, :] = masked * sigmoid(projected[2 * hidden : 3 * hidden]) * projected[3 * hidden :]
    shape = left_ref.shape
    left_ref[...] = a_ref[...].astype(jnp.bfloat16).reshape(shape)
    right_ref[...] = b_ref[...].astype(jnp.bfloat16).reshape(shape)


def make_sides(state, pair_mask, gain, shift, weight):
    rows, cols, channels = state.shape
    hidden = weight.shape[1] // 4
    side = jax.ShapeDtypeStruct((hidden, rows, cols), jnp.bfloat16)
    return pl.pallas_call(
        sides_kernel,
        grid=(rows // ROWS,),
        in_specs=[
            pl.BlockSpec((ROWS, cols, channels), lambda r: (r, 0, 0)),
            pl.BlockSpec((ROWS, cols), lambda r: (r, 0)),
            pl.BlockSpec((1, channels), lambda r: (0, 0)),
            pl.BlockSpec((1, channels), lambda r: (0, 0)),
            pl.BlockSpec((4 * hidden, channels), lambda r: (0, 0)),
        ],
        out_specs=[pl.BlockSpec((hidden, ROWS, cols), lambda r: (0, r, 0))] * 2,
        out_shape=[side, side],
        scratch_shapes=[pltpu.VMEM((hidden * ROWS, cols), jnp.float32)] * 2,
        compiler_params=pltpu.CompilerParams(vmem_limit_bytes=32 * 1024 * 1024),
    )(state, pair_mask, gain[None], shift[None], weight.T)


def update_kernel(
    x_ref, sums_ref, gain_ref, shift_ref, gate_ref, out_gain_ref, out_shift_ref, weight_ref,
    out_ref, t_ref,
):
    hidden = sums_ref.shape[0]
    t_ref[...] = sums_ref[...].reshape(t_ref.shape).astype(jnp.float32)
    for row in range(ROWS):
        widened = x_ref[row].astype(jnp.float32)
        normed = norm_rows(widened, gain_ref[...], shift_ref[...]).astype(jnp.bfloat16)
        gating = sigmoid(
            jnp.dot(normed, gate_ref[...], preferred_element_type=jnp.float32)
        )
        sums = t_ref[pl.ds(row, hidden, stride=ROWS), :]
        center = sums - jnp.mean(sums, axis=0, keepdims=True)
        spread = jnp.mean(center * center, axis=0, keepdims=True)
        scaled = center * lax.rsqrt(spread + EPSILON)
        tri_normed = (scaled * out_gain_ref[...] + out_shift_ref[...]).astype(jnp.bfloat16)
        update = gating * jnp.dot(
            tri_normed.T, weight_ref[...], preferred_element_type=jnp.float32
        )
        out_ref[row] = (widened + update).astype(jnp.bfloat16)


def make_update(state, sums, gain, shift, gate, out_gain, out_shift, weight):
    rows, cols, channels = state.shape
    hidden = sums.shape[0]

    def whole(*dims):
        return pl.BlockSpec(dims, lambda r: (0,) * len(dims))

    return pl.pallas_call(
        update_kernel,
        grid=(rows // ROWS,),
        in_specs=[
            pl.BlockSpec((ROWS, cols, channels), lambda r: (r, 0, 0)),
            pl.BlockSpec((hidden, ROWS, cols), lambda r: (0, r, 0)),
            whole(1, channels),
            whole(1, channels),
            whole(channels, channels),
            whole(hidden, 1),
            whole(hidden, 1),
            whole(hidden, channels),
        ],
        out_specs=pl.BlockSpec((ROWS, cols, channels), lambda r: (r, 0, 0)),
        out_shape=jax.ShapeDtypeStruct(state.shape, jnp.bfloat16),
        scratch_shapes=[pltpu.VMEM((hidden * ROWS, cols), jnp.float32)],
        compiler_params=pltpu.CompilerParams(vmem_limit_bytes=32 * 1024 * 1024),
    )(state, sums, gain[None], shift[None], gate, out_gain[:, None], out_shift[:, None], weight)


def takes_hubs(state, hidden):
    rows, cols, channels = state.shape
    return (
        lax.axis_size("row") == 4
        and lax.axis_size("col") == 4
        and rows == cols
        and rows % 128 == 0
        and channels % 128 == 0
        and hidden % 128 == 0
    )


def triangle_sums(left_side, right_side, outgoing):
    if outgoing:
        return panels_outgoing(left_side, right_side)
    return panels_incoming(left_side, right_side)


def run_pass(
    state,
    pair_mask,
    norm_gain,
    norm_bias,
    proj_weight,
    gate_weight,
    out_gain,
    out_bias,
    out_weight,
    which_pass,
    outgoing,
):
    hidden = out_gain.shape[1]
    if takes_hubs(state, hidden):
        gain, shift = norm_gain[which_pass], norm_bias[which_pass]
        left, right = make_sides(state, pair_mask, gain, shift, proj_weight[which_pass])
        sums = hub_sums(left, right, outgoing)
        return make_update(
            state, sums, gain, shift, gate_weight[which_pass],
            out_gain[which_pass], out_bias[which_pass], out_weight[which_pass],
        )
    widened = state.astype(jnp.float32)
    normed = layer_norm(widened, norm_gain[which_pass], norm_bias[which_pass]).astype(jnp.bfloat16)
    projected = jnp.dot(normed, proj_weight[which_pass], preferred_element_type=jnp.float32)
    masked = pair_mask[:, :, None]
    left_side = (
        masked * jax.nn.sigmoid(projected[:, :, :hidden]) * projected[:, :, hidden : 2 * hidden]
    ).astype(jnp.bfloat16)
    right_side = (
        masked
        * jax.nn.sigmoid(projected[:, :, 2 * hidden : 3 * hidden])
        * projected[:, :, 3 * hidden :]
    ).astype(jnp.bfloat16)
    triangle = triangle_sums(left_side, right_side, outgoing)
    tri_normed = layer_norm(triangle, out_gain[which_pass], out_bias[which_pass]).astype(
        jnp.bfloat16
    )
    gating = jax.nn.sigmoid(
        jnp.dot(normed, gate_weight[which_pass], preferred_element_type=jnp.float32)
    )
    update = gating * jnp.dot(
        tri_normed, out_weight[which_pass], preferred_element_type=jnp.float32
    )
    return (widened + update).astype(jnp.bfloat16)


def local(
    pair,
    chain_ids,
    block_mask,
    norm_gain,
    norm_bias,
    proj_weight,
    gate_weight,
    out_gain,
    out_bias,
    out_weight,
):
    tile_rows, tile_cols = (pair.shape[0], pair.shape[1])
    pair_mask = mask_tile(chain_ids, block_mask, tile_rows, tile_cols)
    middle = run_pass(
        pair,
        pair_mask,
        norm_gain,
        norm_bias,
        proj_weight,
        gate_weight,
        out_gain,
        out_bias,
        out_weight,
        0,
        True,
    )
    return run_pass(
        middle,
        pair_mask,
        norm_gain,
        norm_bias,
        proj_weight,
        gate_weight,
        out_gain,
        out_bias,
        out_weight,
        1,
        False,
    )


def solution(mesh):
    placed = (
        P(("group", "row"), "col", None),
        P("group"),
        P("group", None),
        P(),
        P(),
        P(),
        P(),
        P(),
        P(),
        P(),
    )
    return jax.shard_map(
        local,
        mesh=mesh,
        in_specs=placed,
        out_specs=P(("group", "row"), "col", None),
        check_vma=False,
    )
```

```python
import functools

import jax
import jax.numpy as jnp
from jax import lax
from jax.experimental import pallas as pl
from jax.experimental.pallas import tpu as pltpu
from jax.sharding import PartitionSpec as P

BLOCK = 128


EPSILON = 1e-05


def layer_norm(values, norm_gain, norm_shift):
    center = values - jnp.mean(values, axis=-1, keepdims=True)
    spread = jnp.mean(center * center, axis=-1, keepdims=True)
    return center * lax.rsqrt(spread + EPSILON) * norm_gain + norm_shift


def mask_tile(chain_ids, block_mask, tile_rows, tile_cols):
    row_start = lax.axis_index("row") * tile_rows
    col_start = lax.axis_index("col") * tile_cols
    row_tokens = row_start + jnp.arange(tile_rows, dtype=jnp.int32)
    col_tokens = col_start + jnp.arange(tile_cols, dtype=jnp.int32)
    row_chain = lax.dynamic_slice_in_dim(chain_ids, row_start, tile_rows)
    col_chain = lax.dynamic_slice_in_dim(chain_ids, col_start, tile_cols)
    block_ids = jnp.arange(block_mask.shape[0], dtype=jnp.int32)
    row_onehot = (row_tokens[:, None] // BLOCK == block_ids[None, :]).astype(jnp.float32)
    col_onehot = (col_tokens[:, None] // BLOCK == block_ids[None, :]).astype(jnp.float32)
    row_blocks = jnp.dot(
        row_onehot, block_mask.astype(jnp.float32), precision=lax.Precision.HIGHEST
    )
    block_tile = jnp.dot(row_blocks, col_onehot.T, precision=lax.Precision.HIGHEST)
    same_chain = (row_chain[:, None] == col_chain[None, :]).astype(jnp.float32)
    return jnp.maximum(same_chain, block_tile)


def panels_outgoing(left_side, right_side):
    tile_cols = left_side.shape[1]
    right_panel = lax.all_gather(right_side, "row", axis=0, tiled=True)

    def partial_sum(offset, amount):
        return jnp.einsum(
            "jkh,ikh->jih", right_panel, left_side, preferred_element_type=jnp.float32
        )

    summed = lax.psum_scatter(
        partial_sum(jnp.int32(0), lax.axis_size("col") * tile_cols).astype(jnp.bfloat16),
        "col",
        scatter_dimension=0,
        tiled=True,
    ).astype(jnp.float32)
    return jnp.transpose(summed, (1, 0, 2))


def panels_incoming(left_side, right_side):
    tile_rows = left_side.shape[0]
    left_panel = lax.all_gather(left_side, "col", axis=1, tiled=True)

    def partial_sum(offset, amount):
        return jnp.einsum(
            "kih,kjh->ijh", left_panel, right_side, preferred_element_type=jnp.float32
        )

    return lax.psum_scatter(
        partial_sum(jnp.int32(0), lax.axis_size("row") * tile_rows).astype(jnp.bfloat16),
        "row",
        scatter_dimension=0,
        tiled=True,
    ).astype(jnp.float32)


MESH = pl.DeviceIdType.MESH
CHUNKS = 16


def triangle_kernel(
    outgoing, half, step, moved_ref, fixed_ref, out_ref, moved, fixed, summed, landed, sent,
    ready, local_sem, send_moved, recv_moved, send_fixed, recv_fixed, send_peer, recv_peer,
    send_relay, recv_relay, send_sum, recv_sum, send_out, recv_out,
):
    row, col = lax.axis_index("row"), lax.axis_index("col")
    side, place = row // 2, row % 2
    across, core = col // 2, col % 2
    hub = (row == 1) | (row == 2)
    edge = jnp.logical_not(hub)
    hub_row = side + 1
    end_row = 3 * side
    end_place = side
    hub_place = 1 - side
    other = 1 - core
    pair_at = {"row": row, "col": 2 * across + other}
    if outgoing:
        slot = (row, core)
        held = (place, core)
        mine = across
        peer = [{"row": 3 - row, "col": 2 * across + b} for b in range(2)]
        peer_same = {"row": 3 - row, "col": col}
        sum_peer = {"row": row, "col": 2 * (1 - across) + core}
        moved_pair, fixed_pair = (row, other), (place, other)
        moved_end = [(end_row, b) for b in range(2)]
        fixed_end = [(end_place, b) for b in range(2)]
        moved_peer = [(3 - row, b) for b in range(2)]
    else:
        slot = (col, place)
        held = (core, place)
        mine = side
        peer = [{"row": row, "col": 2 * (1 - across) + b} for b in range(2)]
        peer_same = {"row": row, "col": 2 * (1 - across) + core}
        sum_peer = {"row": 3 - row, "col": col}
        moved_pair, fixed_pair = (2 * across + other, place), (other, place)
        moved_end = [(2 * across + b, end_place) for b in range(2)]
        fixed_end = [(b, end_place) for b in range(2)]
        moved_peer = [(2 * (1 - across) + b, place) for b in range(2)]
    hub_at = [{"row": hub_row, "col": 2 * across + b} for b in range(2)]
    end_at = [{"row": end_row, "col": 2 * across + b} for b in range(2)]

    def remote(source, target, send, recv, device):
        return pltpu.make_async_remote_copy(
            src_ref=source, dst_ref=target, send_sem=send, recv_sem=recv,
            device_id=device, device_id_type=MESH,
        )

    def part(g):
        return pl.ds(g * step, step)

    def span(half_of, g):
        return pl.ds(half_of * half + g * step, step)

    def swap_moved(g):
        return remote(moved_ref.at[span(other, g)], moved.at[slot[0], slot[1], part(g)],
                      send_moved.at[0, g], recv_moved.at[0, g], pair_at)

    def swap_fixed(g):
        return remote(fixed_ref.at[span(other, g)], fixed.at[held[0], held[1], part(g)],
                      send_fixed.at[0, g], recv_fixed.at[0, g], pair_at)

    def end_moved(g, b):
        return remote(moved_ref.at[span(b, g)], moved.at[slot[0], slot[1], part(g)],
                      send_moved.at[b, g], recv_moved.at[1 + core, g], hub_at[b])

    def end_fixed(g, b):
        return remote(fixed_ref.at[span(b, g)], fixed.at[held[0], held[1], part(g)],
                      send_fixed.at[b, g], recv_fixed.at[1 + core, g], hub_at[b])

    def to_peer(g, b):
        return remote(moved_ref.at[span(b, g)], moved.at[slot[0], slot[1], part(g)],
                      send_peer.at[b, g], recv_peer.at[core, g], peer[b])

    def relay_view(g, there):
        if outgoing:
            return moved.at[3 - end_row if there else end_row, :, part(g)]
        start = 2 * (1 - across if there else across)
        return moved.at[pl.ds(start, 2), end_place, part(g)]

    def relay(g):
        return remote(relay_view(g, False), relay_view(g, False),
                      send_relay.at[g], recv_relay.at[g], peer_same)

    def arrived(view, sem):
        remote(view, view, send_relay.at[0], sem, pair_at).wait_recv()

    def sums_to(g):
        return remote(sent.at[g % 2], landed.at[part(g)], send_sum.at[g], recv_sum.at[g], sum_peer)

    def result_pair(g):
        return remote(ready.at[g % 2, hub_place, other], out_ref.at[span(core, g)],
                      send_out.at[2, g], recv_out.at[core, g], pair_at)

    def result_end(g, b):
        return remote(ready.at[g % 2, end_place, b], out_ref.at[span(core, g)],
                      send_out.at[b, g], recv_out.at[core, g], end_at[b])

    barrier = pltpu.get_barrier_semaphore()

    @pl.when(hub)
    def _():
        for device in [pair_at, sum_peer] + end_at + peer:
            pl.semaphore_signal(barrier, inc=1, device_id=device, device_id_type=MESH)
        pl.semaphore_wait(barrier, 6)

    @pl.when(edge)
    def _():
        for device in hub_at:
            pl.semaphore_signal(barrier, inc=1, device_id=device, device_id_type=MESH)
        pl.semaphore_wait(barrier, 2)

    def product(lhs, rhs, dims):
        return lax.dot_general(lhs, rhs, (dims, ((), ())), preferred_element_type=jnp.float32)

    def tiles(group, h):
        for e in range(2):
            if outgoing:
                lhs = [fixed[e, v, h] for v in range(2)]
            else:
                lhs = [moved[2 * group + e, v, h].T for v in range(2)]
            for b in range(2):
                if outgoing:
                    terms = [
                        product(lhs[v], moved[2 * group + b, v, h], ((1,), (1,))) for v in range(2)
                    ]
                else:
                    terms = [product(lhs[v], fixed[b, v, h], ((1,), (0,))) for v in range(2)]
                yield e, b, terms[0] + terms[1]

    @pl.when(edge)
    def _():
        for g in range(CHUNKS):
            if g >= 2:
                for b in range(2):
                    end_moved(g - 2, b).wait_send()
                    end_fixed(g - 2, b).wait_send()
            for b in range(2):
                end_moved(g, b).start()
            for b in range(2):
                end_fixed(g, b).start()
        for g in range(CHUNKS - 2, CHUNKS):
            for b in range(2):
                end_moved(g, b).wait_send()
                end_fixed(g, b).wait_send()
        for g in range(CHUNKS):
            for b in range(2):
                arrived(out_ref.at[span(b, g)], recv_out.at[b, g])

    @pl.when(hub)
    def _():
        own = [
            pltpu.make_async_copy(moved_ref.at[pl.ds(core * half, half)],
                                  moved.at[slot[0], slot[1]], local_sem.at[0]),
            pltpu.make_async_copy(fixed_ref.at[pl.ds(core * half, half)],
                                  fixed.at[held[0], held[1]], local_sem.at[1]),
        ]

        def begin(g):
            for b in range(2):
                to_peer(g, b).start()
            swap_moved(g).start()
            swap_fixed(g).start()

        begin(0)
        for copy in own:
            copy.start()
        begin(1)
        for copy in own:
            copy.wait()
        for g in range(CHUNKS + 2):
            if 2 <= g + 1 < CHUNKS:
                begin(g + 1)
            if g < CHUNKS:
                for b in range(2):
                    u, v = moved_end[b]
                    arrived(moved.at[u, v, part(g)], recv_moved.at[1 + b, g])
                relay(g).start()
            n = g - 1
            if 0 <= n < CHUNKS:
                for b in range(2):
                    u, v = fixed_end[b]
                    arrived(fixed.at[u, v, part(n)], recv_fixed.at[1 + b, n])
                    u, v = moved_peer[b]
                    arrived(moved.at[u, v, part(n)], recv_peer.at[b, n])
                arrived(moved.at[moved_pair[0], moved_pair[1], part(n)], recv_moved.at[0, n])
                arrived(fixed.at[fixed_pair[0], fixed_pair[1], part(n)], recv_fixed.at[0, n])
                arrived(relay_view(n, True), recv_relay.at[n])
                if n >= 2:
                    sums_to(n - 2).wait_send()

                @pl.loop(0, step)
                def _(h):
                    for e, b, total in tiles(1 - mine, n * step + h):
                        sent[n % 2, h, e, b] = total.astype(jnp.bfloat16)

                sums_to(n).start()

                @pl.loop(0, step)
                def _(h):
                    for e, b, total in tiles(mine, n * step + h):
                        summed[n % 2, h, e, b] = total

            n = g - 2
            if 0 <= n < CHUNKS:
                arrived(landed.at[part(n)], recv_sum.at[n])
                if n >= 2:
                    result_pair(n - 2).wait_send()
                    for b in range(2):
                        result_end(n - 2, b).wait_send()

                @pl.loop(0, step)
                def _(h):
                    for e in range(2):
                        for b in range(2):
                            ready[n % 2, e, b, h] = (
                                summed[n % 2, h, e, b]
                                + landed[n * step + h, e, b].astype(jnp.float32)
                            ).astype(jnp.bfloat16)
                    out_ref[core * half + n * step + h] = ready[n % 2, hub_place, core, h]

                for b in range(2):
                    result_end(n, b).start()
                result_pair(n).start()
        for g in range(CHUNKS):
            for b in range(2):
                to_peer(g, b).wait_send()
            swap_moved(g).wait_send()
            swap_fixed(g).wait_send()
            relay(g).wait_send()
        for g in range(CHUNKS - 2, CHUNKS):
            sums_to(g).wait_send()
            result_pair(g).wait_send()
            for b in range(2):
                result_end(g, b).wait_send()
        for g in range(CHUNKS):
            arrived(out_ref.at[span(other, g)], recv_out.at[other, g])


def hub_sums(left_side, right_side, outgoing):
    moved, fixed = (right_side, left_side) if outgoing else (left_side, right_side)
    hidden, edge = moved.shape[0], moved.shape[1]
    half = hidden // 2
    step = half // CHUNKS
    tile = (edge, edge)
    sem = pltpu.SemaphoreType.DMA
    return pl.pallas_call(
        functools.partial(triangle_kernel, outgoing, half, step),
        out_shape=jax.ShapeDtypeStruct(moved.shape, jnp.bfloat16),
        in_specs=[pl.BlockSpec(memory_space=pl.ANY)] * 2,
        out_specs=pl.BlockSpec(memory_space=pltpu.VMEM),
        scratch_shapes=[
            pltpu.VMEM((4, 2, half) + tile, jnp.bfloat16),
            pltpu.VMEM((2, 2, half) + tile, jnp.bfloat16),
            pltpu.VMEM((2, step, 2, 2) + tile, jnp.float32),
            pltpu.VMEM((half, 2, 2) + tile, jnp.bfloat16),
            pltpu.VMEM((2, step, 2, 2) + tile, jnp.bfloat16),
            pltpu.VMEM((2, 2, 2, step) + tile, jnp.bfloat16),
            sem((2,)),
            sem((2, CHUNKS)), sem((3, CHUNKS)),
            sem((2, CHUNKS)), sem((3, CHUNKS)),
            sem((2, CHUNKS)), sem((2, CHUNKS)),
            sem((CHUNKS,)), sem((CHUNKS,)),
            sem((CHUNKS,)), sem((CHUNKS,)),
            sem((3, CHUNKS)), sem((2, CHUNKS)),
        ],
        compiler_params=pltpu.CompilerParams(
            collective_id=0 if outgoing else 1,
            has_side_effects=True,
            vmem_limit_bytes=56 * 1024 * 1024,
        ),
        cost_estimate=pl.CostEstimate(
            flops=32 * hidden * edge**3, bytes_accessed=6 * hidden * edge * edge, transcendentals=0
        ),
    )(moved, fixed)


ROWS = 16


def sigmoid(values):
    return 0.5 * jnp.tanh(0.5 * values) + 0.5


def norm_rows(values, gain, shift):
    center = values - jnp.mean(values, axis=-1, keepdims=True)
    spread = jnp.mean(center * center, axis=-1, keepdims=True)
    return center * lax.rsqrt(spread + EPSILON) * gain + shift


def sides_kernel(x_ref, mask_ref, gain_ref, shift_ref, weight_ref, left_ref, right_ref, a_ref, b_ref):
    hidden = left_ref.shape[0]
    for row in range(ROWS):
        normed = norm_rows(x_ref[row].astype(jnp.float32), gain_ref[...], shift_ref[...])
        projected = lax.dot_general(
            weight_ref[...], normed.astype(jnp.bfloat16), (((1,), (1,)), ((), ())),
            preferred_element_type=jnp.float32,
        )
        masked = mask_ref[row : row + 1, :]
        place = pl.ds(row, hidden, stride=ROWS)
        a_ref[place, :] = masked * sigmoid(projected[:hidden]) * projected[hidden : 2 * hidden]
        b_ref[place, :] = masked * sigmoid(projected[2 * hidden : 3 * hidden]) * projected[3 * hidden :]
    shape = left_ref.shape
    left_ref[...] = a_ref[...].astype(jnp.bfloat16).reshape(shape)
    right_ref[...] = b_ref[...].astype(jnp.bfloat16).reshape(shape)


def make_sides(state, pair_mask, gain, shift, weight):
    rows, cols, channels = state.shape
    hidden = weight.shape[1] // 4
    side = jax.ShapeDtypeStruct((hidden, rows, cols), jnp.bfloat16)
    return pl.pallas_call(
        sides_kernel,
        grid=(rows // ROWS,),
        in_specs=[
            pl.BlockSpec((ROWS, cols, channels), lambda r: (r, 0, 0)),
            pl.BlockSpec((ROWS, cols), lambda r: (r, 0)),
            pl.BlockSpec((1, channels), lambda r: (0, 0)),
            pl.BlockSpec((1, channels), lambda r: (0, 0)),
            pl.BlockSpec((4 * hidden, channels), lambda r: (0, 0)),
        ],
        out_specs=[pl.BlockSpec((hidden, ROWS, cols), lambda r: (0, r, 0))] * 2,
        out_shape=[side, side],
        scratch_shapes=[pltpu.VMEM((hidden * ROWS, cols), jnp.float32)] * 2,
        compiler_params=pltpu.CompilerParams(vmem_limit_bytes=56 * 1024 * 1024),
    )(state, pair_mask, gain[None], shift[None], weight.T)


def update_kernel(
    x_ref, sums_ref, gain_ref, shift_ref, gate_ref, out_gain_ref, out_shift_ref, weight_ref,
    out_ref, t_ref,
):
    hidden = sums_ref.shape[0]
    t_ref[...] = sums_ref[...].reshape(t_ref.shape).astype(jnp.float32)
    for row in range(ROWS):
        widened = x_ref[row].astype(jnp.float32)
        normed = norm_rows(widened, gain_ref[...], shift_ref[...]).astype(jnp.bfloat16)
        gating = sigmoid(
            jnp.dot(normed, gate_ref[...], preferred_element_type=jnp.float32)
        )
        sums = t_ref[pl.ds(row, hidden, stride=ROWS), :]
        center = sums - jnp.mean(sums, axis=0, keepdims=True)
        spread = jnp.mean(center * center, axis=0, keepdims=True)
        scaled = center * lax.rsqrt(spread + EPSILON)
        tri_normed = (scaled * out_gain_ref[...] + out_shift_ref[...]).astype(jnp.bfloat16)
        update = gating * jnp.dot(
            tri_normed.T, weight_ref[...], preferred_element_type=jnp.float32
        )
        out_ref[row] = (widened + update).astype(jnp.bfloat16)


def make_update(state, sums, gain, shift, gate, out_gain, out_shift, weight):
    rows, cols, channels = state.shape
    hidden = sums.shape[0]

    def whole(*dims):
        return pl.BlockSpec(dims, lambda r: (0,) * len(dims))

    return pl.pallas_call(
        update_kernel,
        grid=(rows // ROWS,),
        in_specs=[
            pl.BlockSpec((ROWS, cols, channels), lambda r: (r, 0, 0)),
            pl.BlockSpec((hidden, ROWS, cols), lambda r: (0, r, 0)),
            whole(1, channels),
            whole(1, channels),
            whole(channels, channels),
            whole(hidden, 1),
            whole(hidden, 1),
            whole(hidden, channels),
        ],
        out_specs=pl.BlockSpec((ROWS, cols, channels), lambda r: (r, 0, 0)),
        out_shape=jax.ShapeDtypeStruct(state.shape, jnp.bfloat16),
        scratch_shapes=[pltpu.VMEM((hidden * ROWS, cols), jnp.float32)],
        compiler_params=pltpu.CompilerParams(vmem_limit_bytes=56 * 1024 * 1024),
    )(state, sums, gain[None], shift[None], gate, out_gain[:, None], out_shift[:, None], weight)


def takes_hubs(state, hidden):
    rows, cols, channels = state.shape
    return (
        lax.axis_size("row") == 4
        and lax.axis_size("col") == 4
        and rows == cols
        and rows % 128 == 0
        and channels % 128 == 0
        and hidden % 128 == 0
    )


def triangle_sums(left_side, right_side, outgoing):
    if outgoing:
        return panels_outgoing(left_side, right_side)
    return panels_incoming(left_side, right_side)


def run_pass(
    state,
    pair_mask,
    norm_gain,
    norm_bias,
    proj_weight,
    gate_weight,
    out_gain,
    out_bias,
    out_weight,
    which_pass,
    outgoing,
):
    hidden = out_gain.shape[1]
    if takes_hubs(state, hidden):
        gain, shift = norm_gain[which_pass], norm_bias[which_pass]
        left, right = make_sides(state, pair_mask, gain, shift, proj_weight[which_pass])
        sums = hub_sums(left, right, outgoing)
        return make_update(
            state, sums, gain, shift, gate_weight[which_pass],
            out_gain[which_pass], out_bias[which_pass], out_weight[which_pass],
        )
    widened = state.astype(jnp.float32)
    normed = layer_norm(widened, norm_gain[which_pass], norm_bias[which_pass]).astype(jnp.bfloat16)
    projected = jnp.dot(normed, proj_weight[which_pass], preferred_element_type=jnp.float32)
    masked = pair_mask[:, :, None]
    left_side = (
        masked * jax.nn.sigmoid(projected[:, :, :hidden]) * projected[:, :, hidden : 2 * hidden]
    ).astype(jnp.bfloat16)
    right_side = (
        masked
        * jax.nn.sigmoid(projected[:, :, 2 * hidden : 3 * hidden])
        * projected[:, :, 3 * hidden :]
    ).astype(jnp.bfloat16)
    triangle = triangle_sums(left_side, right_side, outgoing)
    tri_normed = layer_norm(triangle, out_gain[which_pass], out_bias[which_pass]).astype(
        jnp.bfloat16
    )
    gating = jax.nn.sigmoid(
        jnp.dot(normed, gate_weight[which_pass], preferred_element_type=jnp.float32)
    )
    update = gating * jnp.dot(
        tri_normed, out_weight[which_pass], preferred_element_type=jnp.float32
    )
    return (widened + update).astype(jnp.bfloat16)


def local(
    pair,
    chain_ids,
    block_mask,
    norm_gain,
    norm_bias,
    proj_weight,
    gate_weight,
    out_gain,
    out_bias,
    out_weight,
):
    tile_rows, tile_cols = (pair.shape[0], pair.shape[1])
    pair_mask = mask_tile(chain_ids, block_mask, tile_rows, tile_cols)
    middle = run_pass(
        pair,
        pair_mask,
        norm_gain,
        norm_bias,
        proj_weight,
        gate_weight,
        out_gain,
        out_bias,
        out_weight,
        0,
        True,
    )
    return run_pass(
        middle,
        pair_mask,
        norm_gain,
        norm_bias,
        proj_weight,
        gate_weight,
        out_gain,
        out_bias,
        out_weight,
        1,
        False,
    )


def solution(mesh):
    placed = (
        P(("group", "row"), "col", None),
        P("group"),
        P("group", None),
        P(),
        P(),
        P(),
        P(),
        P(),
        P(),
        P(),
    )
    return jax.shard_map(
        local,
        mesh=mesh,
        in_specs=placed,
        out_specs=P(("group", "row"), "col", None),
        check_vma=False,
    )
```

```python
import functools

import jax
import jax.numpy as jnp
from jax import lax
from jax.experimental import pallas as pl
from jax.experimental.pallas import tpu as pltpu
from jax.sharding import PartitionSpec as P

BLOCK = 128


EPSILON = 1e-05


def layer_norm(values, norm_gain, norm_shift):
    center = values - jnp.mean(values, axis=-1, keepdims=True)
    spread = jnp.mean(center * center, axis=-1, keepdims=True)
    return center * lax.rsqrt(spread + EPSILON) * norm_gain + norm_shift


def mask_tile(chain_ids, block_mask, tile_rows, tile_cols):
    row_start = lax.axis_index("row") * tile_rows
    col_start = lax.axis_index("col") * tile_cols
    row_tokens = row_start + jnp.arange(tile_rows, dtype=jnp.int32)
    col_tokens = col_start + jnp.arange(tile_cols, dtype=jnp.int32)
    row_chain = lax.dynamic_slice_in_dim(chain_ids, row_start, tile_rows)
    col_chain = lax.dynamic_slice_in_dim(chain_ids, col_start, tile_cols)
    block_ids = jnp.arange(block_mask.shape[0], dtype=jnp.int32)
    row_onehot = (row_tokens[:, None] // BLOCK == block_ids[None, :]).astype(jnp.float32)
    col_onehot = (col_tokens[:, None] // BLOCK == block_ids[None, :]).astype(jnp.float32)
    row_blocks = jnp.dot(
        row_onehot, block_mask.astype(jnp.float32), precision=lax.Precision.HIGHEST
    )
    block_tile = jnp.dot(row_blocks, col_onehot.T, precision=lax.Precision.HIGHEST)
    same_chain = (row_chain[:, None] == col_chain[None, :]).astype(jnp.float32)
    return jnp.maximum(same_chain, block_tile)


def panels_outgoing(left_side, right_side):
    tile_cols = left_side.shape[1]
    right_panel = lax.all_gather(right_side, "row", axis=0, tiled=True)

    def partial_sum(offset, amount):
        return jnp.einsum(
            "jkh,ikh->jih", right_panel, left_side, preferred_element_type=jnp.float32
        )

    summed = lax.psum_scatter(
        partial_sum(jnp.int32(0), lax.axis_size("col") * tile_cols).astype(jnp.bfloat16),
        "col",
        scatter_dimension=0,
        tiled=True,
    ).astype(jnp.float32)
    return jnp.transpose(summed, (1, 0, 2))


def panels_incoming(left_side, right_side):
    tile_rows = left_side.shape[0]
    left_panel = lax.all_gather(left_side, "col", axis=1, tiled=True)

    def partial_sum(offset, amount):
        return jnp.einsum(
            "kih,kjh->ijh", left_panel, right_side, preferred_element_type=jnp.float32
        )

    return lax.psum_scatter(
        partial_sum(jnp.int32(0), lax.axis_size("row") * tile_rows).astype(jnp.bfloat16),
        "row",
        scatter_dimension=0,
        tiled=True,
    ).astype(jnp.float32)


MESH = pl.DeviceIdType.MESH
CHUNKS = 32


def triangle_kernel(
    outgoing, half, step, moved_ref, fixed_ref, out_ref, moved, fixed, summed, landed, sent,
    ready, local_sem, send_moved, recv_moved, send_fixed, recv_fixed, send_peer, recv_peer,
    send_relay, recv_relay, send_sum, recv_sum, send_out, recv_out,
):
    row, col = lax.axis_index("row"), lax.axis_index("col")
    side, place = row // 2, row % 2
    across, core = col // 2, col % 2
    hub = (row == 1) | (row == 2)
    edge = jnp.logical_not(hub)
    hub_row = side + 1
    end_row = 3 * side
    end_place = side
    hub_place = 1 - side
    other = 1 - core
    pair_at = {"row": row, "col": 2 * across + other}
    if outgoing:
        slot = (row, core)
        held = (place, core)
        mine = across
        peer = [{"row": 3 - row, "col": 2 * across + b} for b in range(2)]
        peer_same = {"row": 3 - row, "col": col}
        sum_peer = {"row": row, "col": 2 * (1 - across) + core}
        moved_pair, fixed_pair = (row, other), (place, other)
        moved_end = [(end_row, b) for b in range(2)]
        fixed_end = [(end_place, b) for b in range(2)]
        moved_peer = [(3 - row, b) for b in range(2)]
    else:
        slot = (col, place)
        held = (core, place)
        mine = side
        peer = [{"row": row, "col": 2 * (1 - across) + b} for b in range(2)]
        peer_same = {"row": row, "col": 2 * (1 - across) + core}
        sum_peer = {"row": 3 - row, "col": col}
        moved_pair, fixed_pair = (2 * across + other, place), (other, place)
        moved_end = [(2 * across + b, end_place) for b in range(2)]
        fixed_end = [(b, end_place) for b in range(2)]
        moved_peer = [(2 * (1 - across) + b, place) for b in range(2)]
    hub_at = [{"row": hub_row, "col": 2 * across + b} for b in range(2)]
    end_at = [{"row": end_row, "col": 2 * across + b} for b in range(2)]

    def remote(source, target, send, recv, device):
        return pltpu.make_async_remote_copy(
            src_ref=source, dst_ref=target, send_sem=send, recv_sem=recv,
            device_id=device, device_id_type=MESH,
        )

    def part(g):
        return pl.ds(g * step, step)

    def span(half_of, g):
        return pl.ds(half_of * half + g * step, step)

    def swap_moved(g):
        return remote(moved_ref.at[span(other, g)], moved.at[slot[0], slot[1], part(g)],
                      send_moved.at[0, g], recv_moved.at[0, g], pair_at)

    def swap_fixed(g):
        return remote(fixed_ref.at[span(other, g)], fixed.at[held[0], held[1], part(g)],
                      send_fixed.at[0, g], recv_fixed.at[0, g], pair_at)

    def end_moved(g, b):
        return remote(moved_ref.at[span(b, g)], moved.at[slot[0], slot[1], part(g)],
                      send_moved.at[b, g], recv_moved.at[1 + core, g], hub_at[b])

    def end_fixed(g, b):
        return remote(fixed_ref.at[span(b, g)], fixed.at[held[0], held[1], part(g)],
                      send_fixed.at[b, g], recv_fixed.at[1 + core, g], hub_at[b])

    def to_peer(g, b):
        return remote(moved_ref.at[span(b, g)], moved.at[slot[0], slot[1], part(g)],
                      send_peer.at[b, g], recv_peer.at[core, g], peer[b])

    def relay_view(g, there):
        if outgoing:
            return moved.at[3 - end_row if there else end_row, :, part(g)]
        start = 2 * (1 - across if there else across)
        return moved.at[pl.ds(start, 2), end_place, part(g)]

    def relay(g):
        return remote(relay_view(g, False), relay_view(g, False),
                      send_relay.at[g], recv_relay.at[g], peer_same)

    def arrived(view, sem):
        remote(view, view, send_relay.at[0], sem, pair_at).wait_recv()

    def sums_to(g):
        return remote(sent.at[g % 2], landed.at[part(g)], send_sum.at[g], recv_sum.at[g], sum_peer)

    def result_pair(g):
        return remote(ready.at[g % 2, hub_place, other], out_ref.at[span(core, g)],
                      send_out.at[2, g], recv_out.at[core, g], pair_at)

    def result_end(g, b):
        return remote(ready.at[g % 2, end_place, b], out_ref.at[span(core, g)],
                      send_out.at[b, g], recv_out.at[core, g], end_at[b])

    barrier = pltpu.get_barrier_semaphore()

    @pl.when(hub)
    def _():
        for device in [pair_at, sum_peer] + end_at + peer:
            pl.semaphore_signal(barrier, inc=1, device_id=device, device_id_type=MESH)
        pl.semaphore_wait(barrier, 6)

    @pl.when(edge)
    def _():
        for device in hub_at:
            pl.semaphore_signal(barrier, inc=1, device_id=device, device_id_type=MESH)
        pl.semaphore_wait(barrier, 2)

    def product(lhs, rhs, dims):
        return lax.dot_general(lhs, rhs, (dims, ((), ())), preferred_element_type=jnp.float32)

    def tiles(group, h):
        for e in range(2):
            if outgoing:
                lhs = [fixed[e, v, h] for v in range(2)]
            else:
                lhs = [moved[2 * group + e, v, h].T for v in range(2)]
            for b in range(2):
                if outgoing:
                    terms = [
                        product(lhs[v], moved[2 * group + b, v, h], ((1,), (1,))) for v in range(2)
                    ]
                else:
                    terms = [product(lhs[v], fixed[b, v, h], ((1,), (0,))) for v in range(2)]
                yield e, b, terms[0] + terms[1]

    @pl.when(edge)
    def _():
        for g in range(CHUNKS):
            if g >= 4:
                for b in range(2):
                    end_moved(g - 4, b).wait_send()
                    end_fixed(g - 4, b).wait_send()
            for b in range(2):
                end_moved(g, b).start()
            for b in range(2):
                end_fixed(g, b).start()
        for g in range(CHUNKS - 4, CHUNKS):
            for b in range(2):
                end_moved(g, b).wait_send()
                end_fixed(g, b).wait_send()
        for g in range(CHUNKS):
            for b in range(2):
                arrived(out_ref.at[span(b, g)], recv_out.at[b, g])

    @pl.when(hub)
    def _():
        own = [
            pltpu.make_async_copy(moved_ref.at[pl.ds(core * half, half)],
                                  moved.at[slot[0], slot[1]], local_sem.at[0]),
            pltpu.make_async_copy(fixed_ref.at[pl.ds(core * half, half)],
                                  fixed.at[held[0], held[1]], local_sem.at[1]),
        ]

        def begin(g):
            for b in range(2):
                to_peer(g, b).start()
            swap_moved(g).start()
            swap_fixed(g).start()

        begin(0)
        for copy in own:
            copy.start()
        begin(1)
        for copy in own:
            copy.wait()
        for g in range(CHUNKS + 2):
            if 2 <= g + 1 < CHUNKS:
                begin(g + 1)
            if g < CHUNKS:
                for b in range(2):
                    u, v = moved_end[b]
                    arrived(moved.at[u, v, part(g)], recv_moved.at[1 + b, g])
                relay(g).start()
            n = g - 1
            if 0 <= n < CHUNKS:
                for b in range(2):
                    u, v = fixed_end[b]
                    arrived(fixed.at[u, v, part(n)], recv_fixed.at[1 + b, n])
                    u, v = moved_peer[b]
                    arrived(moved.at[u, v, part(n)], recv_peer.at[b, n])
                arrived(moved.at[moved_pair[0], moved_pair[1], part(n)], recv_moved.at[0, n])
                arrived(fixed.at[fixed_pair[0], fixed_pair[1], part(n)], recv_fixed.at[0, n])
                arrived(relay_view(n, True), recv_relay.at[n])
                if n >= 2:
                    sums_to(n - 2).wait_send()

                @pl.loop(0, step)
                def _(h):
                    for e, b, total in tiles(1 - mine, n * step + h):
                        sent[n % 2, h, e, b] = total.astype(jnp.bfloat16)

                sums_to(n).start()

                @pl.loop(0, step)
                def _(h):
                    for e, b, total in tiles(mine, n * step + h):
                        summed[n % 2, h, e, b] = total

            n = g - 2
            if 0 <= n < CHUNKS:
                arrived(landed.at[part(n)], recv_sum.at[n])
                if n >= 2:
                    result_pair(n - 2).wait_send()
                    for b in range(2):
                        result_end(n - 2, b).wait_send()

                @pl.loop(0, step)
                def _(h):
                    for e in range(2):
                        for b in range(2):
                            ready[n % 2, e, b, h] = (
                                summed[n % 2, h, e, b]
                                + landed[n * step + h, e, b].astype(jnp.float32)
                            ).astype(jnp.bfloat16)
                    out_ref[core * half + n * step + h] = ready[n % 2, hub_place, core, h]

                for b in range(2):
                    result_end(n, b).start()
                result_pair(n).start()
        for g in range(CHUNKS):
            for b in range(2):
                to_peer(g, b).wait_send()
            swap_moved(g).wait_send()
            swap_fixed(g).wait_send()
            relay(g).wait_send()
        for g in range(CHUNKS - 2, CHUNKS):
            sums_to(g).wait_send()
            result_pair(g).wait_send()
            for b in range(2):
                result_end(g, b).wait_send()
        for g in range(CHUNKS):
            arrived(out_ref.at[span(other, g)], recv_out.at[other, g])


def hub_sums(left_side, right_side, outgoing):
    moved, fixed = (right_side, left_side) if outgoing else (left_side, right_side)
    hidden, edge = moved.shape[0], moved.shape[1]
    half = hidden // 2
    step = half // CHUNKS
    tile = (edge, edge)
    sem = pltpu.SemaphoreType.DMA
    return pl.pallas_call(
        functools.partial(triangle_kernel, outgoing, half, step),
        out_shape=jax.ShapeDtypeStruct(moved.shape, jnp.bfloat16),
        in_specs=[pl.BlockSpec(memory_space=pl.ANY)] * 2,
        out_specs=pl.BlockSpec(memory_space=pltpu.VMEM),
        scratch_shapes=[
            pltpu.VMEM((4, 2, half) + tile, jnp.bfloat16),
            pltpu.VMEM((2, 2, half) + tile, jnp.bfloat16),
            pltpu.VMEM((2, step, 2, 2) + tile, jnp.float32),
            pltpu.VMEM((half, 2, 2) + tile, jnp.bfloat16),
            pltpu.VMEM((2, step, 2, 2) + tile, jnp.bfloat16),
            pltpu.VMEM((2, 2, 2, step) + tile, jnp.bfloat16),
            sem((2,)),
            sem((2, CHUNKS)), sem((3, CHUNKS)),
            sem((2, CHUNKS)), sem((3, CHUNKS)),
            sem((2, CHUNKS)), sem((2, CHUNKS)),
            sem((CHUNKS,)), sem((CHUNKS,)),
            sem((CHUNKS,)), sem((CHUNKS,)),
            sem((3, CHUNKS)), sem((2, CHUNKS)),
        ],
        compiler_params=pltpu.CompilerParams(
            collective_id=0 if outgoing else 1,
            has_side_effects=True,
            vmem_limit_bytes=56 * 1024 * 1024,
        ),
        cost_estimate=pl.CostEstimate(
            flops=32 * hidden * edge**3, bytes_accessed=6 * hidden * edge * edge, transcendentals=0
        ),
    )(moved, fixed)


ROWS = 16


def sigmoid(values):
    return 0.5 * jnp.tanh(0.5 * values) + 0.5


def norm_rows(values, gain, shift):
    center = values - jnp.mean(values, axis=-1, keepdims=True)
    spread = jnp.mean(center * center, axis=-1, keepdims=True)
    return center * lax.rsqrt(spread + EPSILON) * gain + shift


def sides_kernel(x_ref, mask_ref, gain_ref, shift_ref, weight_ref, left_ref, right_ref, a_ref, b_ref):
    hidden = left_ref.shape[0]
    for row in range(ROWS):
        normed = norm_rows(x_ref[row].astype(jnp.float32), gain_ref[...], shift_ref[...])
        projected = lax.dot_general(
            weight_ref[...], normed.astype(jnp.bfloat16), (((1,), (1,)), ((), ())),
            preferred_element_type=jnp.float32,
        )
        masked = mask_ref[row : row + 1, :]
        place = pl.ds(row, hidden, stride=ROWS)
        a_ref[place, :] = masked * sigmoid(projected[:hidden]) * projected[hidden : 2 * hidden]
        b_ref[place, :] = masked * sigmoid(projected[2 * hidden : 3 * hidden]) * projected[3 * hidden :]
    shape = left_ref.shape
    left_ref[...] = a_ref[...].astype(jnp.bfloat16).reshape(shape)
    right_ref[...] = b_ref[...].astype(jnp.bfloat16).reshape(shape)


def make_sides(state, pair_mask, gain, shift, weight):
    rows, cols, channels = state.shape
    hidden = weight.shape[1] // 4
    side = jax.ShapeDtypeStruct((hidden, rows, cols), jnp.bfloat16)
    return pl.pallas_call(
        sides_kernel,
        grid=(rows // ROWS,),
        in_specs=[
            pl.BlockSpec((ROWS, cols, channels), lambda r: (r, 0, 0)),
            pl.BlockSpec((ROWS, cols), lambda r: (r, 0)),
            pl.BlockSpec((1, channels), lambda r: (0, 0)),
            pl.BlockSpec((1, channels), lambda r: (0, 0)),
            pl.BlockSpec((4 * hidden, channels), lambda r: (0, 0)),
        ],
        out_specs=[pl.BlockSpec((hidden, ROWS, cols), lambda r: (0, r, 0))] * 2,
        out_shape=[side, side],
        scratch_shapes=[pltpu.VMEM((hidden * ROWS, cols), jnp.float32)] * 2,
        compiler_params=pltpu.CompilerParams(vmem_limit_bytes=56 * 1024 * 1024),
    )(state, pair_mask, gain[None], shift[None], weight.T)


def update_kernel(
    x_ref, sums_ref, gain_ref, shift_ref, gate_ref, out_gain_ref, out_shift_ref, weight_ref,
    out_ref, t_ref,
):
    hidden = sums_ref.shape[0]
    t_ref[...] = sums_ref[...].reshape(t_ref.shape).astype(jnp.float32)
    for row in range(ROWS):
        widened = x_ref[row].astype(jnp.float32)
        normed = norm_rows(widened, gain_ref[...], shift_ref[...]).astype(jnp.bfloat16)
        gating = sigmoid(
            jnp.dot(normed, gate_ref[...], preferred_element_type=jnp.float32)
        )
        sums = t_ref[pl.ds(row, hidden, stride=ROWS), :]
        center = sums - jnp.mean(sums, axis=0, keepdims=True)
        spread = jnp.mean(center * center, axis=0, keepdims=True)
        scaled = center * lax.rsqrt(spread + EPSILON)
        tri_normed = (scaled * out_gain_ref[...] + out_shift_ref[...]).astype(jnp.bfloat16)
        update = gating * jnp.dot(
            tri_normed.T, weight_ref[...], preferred_element_type=jnp.float32
        )
        out_ref[row] = (widened + update).astype(jnp.bfloat16)


def make_update(state, sums, gain, shift, gate, out_gain, out_shift, weight):
    rows, cols, channels = state.shape
    hidden = sums.shape[0]

    def whole(*dims):
        return pl.BlockSpec(dims, lambda r: (0,) * len(dims))

    return pl.pallas_call(
        update_kernel,
        grid=(rows // ROWS,),
        in_specs=[
            pl.BlockSpec((ROWS, cols, channels), lambda r: (r, 0, 0)),
            pl.BlockSpec((hidden, ROWS, cols), lambda r: (0, r, 0)),
            whole(1, channels),
            whole(1, channels),
            whole(channels, channels),
            whole(hidden, 1),
            whole(hidden, 1),
            whole(hidden, channels),
        ],
        out_specs=pl.BlockSpec((ROWS, cols, channels), lambda r: (r, 0, 0)),
        out_shape=jax.ShapeDtypeStruct(state.shape, jnp.bfloat16),
        scratch_shapes=[pltpu.VMEM((hidden * ROWS, cols), jnp.float32)],
        compiler_params=pltpu.CompilerParams(vmem_limit_bytes=56 * 1024 * 1024),
    )(state, sums, gain[None], shift[None], gate, out_gain[:, None], out_shift[:, None], weight)


def takes_hubs(state, hidden):
    rows, cols, channels = state.shape
    return (
        lax.axis_size("row") == 4
        and lax.axis_size("col") == 4
        and rows == cols
        and rows % 128 == 0
        and channels % 128 == 0
        and hidden % 128 == 0
    )


def triangle_sums(left_side, right_side, outgoing):
    if outgoing:
        return panels_outgoing(left_side, right_side)
    return panels_incoming(left_side, right_side)


def run_pass(
    state,
    pair_mask,
    norm_gain,
    norm_bias,
    proj_weight,
    gate_weight,
    out_gain,
    out_bias,
    out_weight,
    which_pass,
    outgoing,
):
    hidden = out_gain.shape[1]
    if takes_hubs(state, hidden):
        gain, shift = norm_gain[which_pass], norm_bias[which_pass]
        left, right = make_sides(state, pair_mask, gain, shift, proj_weight[which_pass])
        sums = hub_sums(left, right, outgoing)
        return make_update(
            state, sums, gain, shift, gate_weight[which_pass],
            out_gain[which_pass], out_bias[which_pass], out_weight[which_pass],
        )
    widened = state.astype(jnp.float32)
    normed = layer_norm(widened, norm_gain[which_pass], norm_bias[which_pass]).astype(jnp.bfloat16)
    projected = jnp.dot(normed, proj_weight[which_pass], preferred_element_type=jnp.float32)
    masked = pair_mask[:, :, None]
    left_side = (
        masked * jax.nn.sigmoid(projected[:, :, :hidden]) * projected[:, :, hidden : 2 * hidden]
    ).astype(jnp.bfloat16)
    right_side = (
        masked
        * jax.nn.sigmoid(projected[:, :, 2 * hidden : 3 * hidden])
        * projected[:, :, 3 * hidden :]
    ).astype(jnp.bfloat16)
    triangle = triangle_sums(left_side, right_side, outgoing)
    tri_normed = layer_norm(triangle, out_gain[which_pass], out_bias[which_pass]).astype(
        jnp.bfloat16
    )
    gating = jax.nn.sigmoid(
        jnp.dot(normed, gate_weight[which_pass], preferred_element_type=jnp.float32)
    )
    update = gating * jnp.dot(
        tri_normed, out_weight[which_pass], preferred_element_type=jnp.float32
    )
    return (widened + update).astype(jnp.bfloat16)


def local(
    pair,
    chain_ids,
    block_mask,
    norm_gain,
    norm_bias,
    proj_weight,
    gate_weight,
    out_gain,
    out_bias,
    out_weight,
):
    tile_rows, tile_cols = (pair.shape[0], pair.shape[1])
    pair_mask = mask_tile(chain_ids, block_mask, tile_rows, tile_cols)
    middle = run_pass(
        pair,
        pair_mask,
        norm_gain,
        norm_bias,
        proj_weight,
        gate_weight,
        out_gain,
        out_bias,
        out_weight,
        0,
        True,
    )
    return run_pass(
        middle,
        pair_mask,
        norm_gain,
        norm_bias,
        proj_weight,
        gate_weight,
        out_gain,
        out_bias,
        out_weight,
        1,
        False,
    )


def solution(mesh):
    placed = (
        P(("group", "row"), "col", None),
        P("group"),
        P("group", None),
        P(),
        P(),
        P(),
        P(),
        P(),
        P(),
        P(),
    )
    return jax.shard_map(
        local,
        mesh=mesh,
        in_specs=placed,
        out_specs=P(("group", "row"), "col", None),
        check_vma=False,
    )
```
